256 devices in a mesh: dp: 64 (over x, z_hi, y), ctx: 4 (over z_lo, core).
Axes of the slice: x: 4, y: 4, z: 8 (z_hi: 4, z_lo: 2; z = z_hi * 2 + z_lo), core: 2. Of those that a mesh axis runs over, the one named last changes fastest.
Arguments:
- queries: bfloat16 [64, 1024, 4096], P('dp', 'ctx'), may hold values from -90 to 90
- keys: bfloat16 [64, 1024, 512], P('dp', 'ctx'), may hold values from -9 to 9
- values: bfloat16 [64, 1024, 512], P('dp', 'ctx'), may hold values from -6 to 6
- segment_ids: int32 [64, 1024], P('dp', 'ctx'), may hold values from 0 to 7, never falling along the last dimension, each value on 1 to 512 neighbouring positions
- out_grad: bfloat16 [64, 1024, 4096], P('dp', 'ctx'), may hold values from -6 to 6
- partner_bit: int32 [1], replicated, may hold values from 0 to 2
Outputs:
- attn_out: bfloat16 [64, 1024, 4096], P('dp', 'ctx')
- grad_q: bfloat16 [64, 1024, 4096], P('dp', 'ctx')
- grad_k: bfloat16 [64, 1024, 512], P('dp', 'ctx')
- grad_v: bfloat16 [64, 1024, 512], P('dp', 'ctx')
The draws below stay inside these ranges and needn't reach their ends.
Inputs may be any that keep to these rules, and one draw needn't show every extreme that they name: partner(s) = s XOR 2 ** partner_bit[0] pairs the sequences.
All inputs are finite; a program needn't handle non-finite values.
Results may differ from the reference program's by a relative error of at most 0.035.
Values may be sent and summed in bfloat16 or wider, within the bound.
No kernel may reach another device: no remote copies, remote signals or barrier semaphores. Data moves between devices by JAX's collectives and lax.ppermute only.
A program may use at most 192 MiB of HBM per device.

```python
import math
import jax
import jax.numpy as jnp
import numpy as np
from jax import lax

HEADS = 32
KV_HEADS = 4
HEAD_DIM = 128
SEQ_LEN = 1024
SEQS = 64


def shared_base(key):
    base = jax.random.normal(key, (SEQS, SEQ_LEN, KV_HEADS, HEAD_DIM), jnp.float32)
    return jnp.clip(base, -6.0, 6.0)


def draw_keys(key, part):
    base = shared_base(key)
    return base.reshape(SEQS, SEQ_LEN, KV_HEADS * HEAD_DIM).astype(jnp.bfloat16)


def draw_queries(key, part):
    key = jax.random.fold_in(key, 7)
    shape = (SEQS, SEQ_LEN, HEADS, HEAD_DIM)
    own = jnp.clip(jax.random.normal(key, shape, jnp.float32), -6.0, 6.0)
    return own.reshape(SEQS, SEQ_LEN, HEADS * HEAD_DIM).astype(jnp.bfloat16)


def steps_of(key, dims, split, smallest, largest):
    def one(position, parts):
        draws = jax.random.uniform(jax.random.fold_in(jax.random.fold_in(key, 6), position), (parts,), jnp.float32, smallest / len(split), largest / len(split))
        return jnp.repeat(jnp.exp(draws), dims[position] // parts).reshape((-1,) + (1,) * (len(dims) - position - 1))

    gain = one(*split[0])
    for cut in split[1:]:
        gain = gain * one(*cut)
    return gain


def length_profile(number_of, total, bound, lean):
    loads = [(1 << 20) // math.isqrt(standing ** lean) + 1 for standing in range(2, number_of + 1)]
    surplus, counts = total - bound - (number_of - 1), [1] * (number_of - 1)
    while surplus > 0:
        free = [i for i in range(number_of - 1) if counts[i] < bound]
        pool, budget = sum([loads[i] for i in free]), surplus
        for i in free:
            more = min(bound - counts[i], max(1, budget * loads[i] // pool), surplus)
            counts[i] = counts[i] + more
            surplus = surplus - more
    return np.array([bound] + counts)


def uneven(stream_key, amount, total, bound, lean):
    if amount == 2:
        one = jax.random.randint(stream_key, (), max(1, total - bound), min(bound, total - 1) + 1)
        return jnp.stack([one, total - one])
    lengths = jnp.asarray(length_profile(amount, total, bound, lean), jnp.int32)
    pairs = (amount - 1) // 2
    source_of, receiver = lengths[1:1 + 2 * pairs:2], lengths[2:2 + 2 * pairs:2]
    slack = jnp.minimum(source_of - 1, bound - receiver)
    passed = jax.random.randint(jax.random.fold_in(stream_key, 1), (pairs,), 0, 1 << 20) % (slack + 1)
    lengths = lengths.at[1:1 + 2 * pairs:2].set(source_of - passed).at[2:2 + 2 * pairs:2].set(receiver + passed)
    return lengths[jax.random.permutation(jax.random.fold_in(stream_key, 2), amount)]


def normal_values(rng, dims, scale, most, cuts=(), kind=jnp.bfloat16):
    gain = steps_of(rng, dims, cuts, -0.22, 0.18) if cuts else 1.0
    values = jax.random.normal(rng, dims, jnp.float32) * scale * gain
    return jnp.minimum(jnp.maximum(values, -most), most).astype(kind)


def setup_inputs(seed: int = 0) -> dict:
    splits = jax.random.split(jax.random.key(seed), 7)
    return {
        "queries": draw_queries(jax.random.fold_in(splits[6], 71), 0),
        "keys": draw_keys(jax.random.fold_in(splits[6], 71), 0),
        "values": normal_values(splits[2], (SEQS, SEQ_LEN, KV_HEADS * HEAD_DIM), 1.0, 6.0, ((0, 64), (1, 4))),
        "segment_ids": jax.vmap(lambda own: jnp.searchsorted(jnp.cumsum(uneven(own, max(SEQ_LEN // 128, 3), SEQ_LEN, SEQ_LEN // 2, 2)), jnp.arange(SEQ_LEN), side="right"))(jax.random.split(splits[3], SEQS)).reshape((SEQS, SEQ_LEN)).astype(jnp.int32),
        "out_grad": normal_values(splits[4], (SEQS, SEQ_LEN, HEADS * HEAD_DIM), 1.0, 6.0, ((0, 64), (1, 4))),
        "partner_bit": jax.random.randint(splits[5], (1,), 0, 3).astype(jnp.int32),
    }


def one_sequence(qrow, krow, vrow, segrow, cotrow):
    length = qrow.shape[0]
    group = HEADS // KV_HEADS
    scale = HEAD_DIM ** -0.5
    qf = qrow.astype(jnp.float32).reshape(length, KV_HEADS, group, HEAD_DIM)
    kf = krow.astype(jnp.float32).reshape(length, KV_HEADS, HEAD_DIM)
    vf = vrow.astype(jnp.float32).reshape(length, KV_HEADS, HEAD_DIM)
    scores = jnp.einsum("qkgd,nkd->kgqn", qf, kf) * scale
    positions = jnp.arange(length, dtype=jnp.int32)
    allowed = (segrow[:, None] == segrow[None, :]) & (positions[None, :] <= positions[:, None])
    scores = jnp.where(allowed, scores, jnp.float32(-1e30))
    top = jnp.max(scores, axis=-1, keepdims=True)
    raw = jnp.where(allowed, jnp.exp(scores - top), jnp.float32(0.0))
    weights = raw / jnp.sum(raw, axis=-1, keepdims=True)
    weights_b = weights.astype(jnp.bfloat16).astype(jnp.float32)
    own = jnp.einsum("kgqn,nkd->qkgd", weights_b, vf).astype(jnp.bfloat16)
    cot = cotrow.astype(jnp.float32).reshape(length, KV_HEADS, group, HEAD_DIM)
    delta = jnp.transpose(jnp.sum(cot * own.astype(jnp.float32), axis=-1), (1, 2, 0))
    grad_v = jnp.einsum("kgqn,qkgd->nkd", weights_b, cot)
    dweights = jnp.einsum("qkgd,nkd->kgqn", cot, vf)
    dscores = (weights * (dweights - delta[..., None])).astype(jnp.bfloat16).astype(jnp.float32)
    grad_q = jnp.einsum("kgqn,nkd->qkgd", dscores, kf) * scale
    grad_k = jnp.einsum("kgqn,qkgd->nkd", dscores, qf) * scale
    return (own.reshape(length, HEADS * HEAD_DIM),
            grad_q.reshape(length, HEADS * HEAD_DIM).astype(jnp.bfloat16),
            grad_k.reshape(length, KV_HEADS * HEAD_DIM).astype(jnp.bfloat16),
            grad_v.reshape(length, KV_HEADS * HEAD_DIM).astype(jnp.bfloat16))


def reference(queries, keys, values, segment_ids, out_grad, partner_bit):
    order = jnp.arange(SEQS, dtype=jnp.int32)
    partner = jnp.bitwise_xor(order, jnp.left_shift(jnp.int32(1), partner_bit[0].astype(jnp.int32)))

    def per_sequence(index):
        other = partner[index]
        return one_sequence(queries[index], keys[index], values[index], segment_ids[index], out_grad[other])

    own, grad_q, grad_k, grad_v = lax.map(per_sequence, order)
    attn_out = jnp.take(own, partner, axis=0)
    return attn_out, grad_q, grad_k, grad_v
```

```python
from functools import partial

import jax
import jax.numpy as jnp
from jax import lax
from jax.experimental import pallas as pl
from jax.experimental.pallas import tpu as pltpu
from jax.sharding import PartitionSpec as P

HEADS = 32
KV_HEADS = 4
GROUP = HEADS // KV_HEADS
DIM = 128
ROWS = 256
TILE = 128
BAND = 640
WINDOW = 768
HP = 2
KV_COLS = KV_HEADS * DIM
LOG2E = 1.4426950408889634
SCALE = DIM**-0.5
MASKED = -1e30
PARTS = ((0, 3), (3, 1))
VMEM = 48 * 1024 * 1024

NT = (((1,), (1,)), ((), ()))
NN = (((1,), (0,)), ((), ()))


def dot(a, b, dims):
    return lax.dot_general(a, b, dims, preferred_element_type=jnp.float32)


def band(refs, first):
    return jnp.concatenate([ref[...] for ref in refs], axis=0)[first : first + BAND]


def bias_of(seg_refs, segq_ref, tile):
    segk = band(seg_refs, tile * TILE).astype(jnp.float32)
    segq = segq_ref[:, tile * TILE : (tile + 1) * TILE]
    key = lax.broadcasted_iota(jnp.int32, (BAND, TILE), 0)
    query = lax.broadcasted_iota(jnp.int32, (BAND, TILE), 1) + (BAND - TILE)
    ok = (segk == segq) & (key <= query)
    bias = jnp.where(ok, jnp.float32(0.0), jnp.float32(MASKED))
    return jnp.concatenate([bias] * HP, axis=1)


def head_cols(head):
    return slice(head * DIM, (head + 1) * DIM)


def heads_of(ref, tile, first, count=HP):
    rows = slice(tile * TILE, (tile + 1) * TILE)
    return jnp.concatenate([ref[rows, head_cols(first + n)] for n in range(count)], axis=0)


def put_heads(ref, tile, first, value):
    rows = slice(tile * TILE, (tile + 1) * TILE)
    for n in range(HP):
        ref[rows, head_cols(first + n)] = value[n * TILE : (n + 1) * TILE].astype(ref.dtype)


def over_heads(step):
    for first in range(0, GROUP, HP):
        step(first)


def forward_kernel(q, k2, v2, s2, k1, v1, s1, k0, v0, s0, segq, out, lse):
    for tile in range(ROWS // TILE):
        k = band((k2, k1, k0), tile * TILE)
        vt = band((v2, v1, v0), tile * TILE).T
        bias = bias_of((s2, s1, s0), segq, tile)

        def step(first):
            x = dot(k, heads_of(q, tile, first), NT) * (SCALE * LOG2E) + bias
            top = jnp.max(x, axis=0, keepdims=True)
            p = jnp.exp2(x - top)
            total = jnp.sum(p, axis=0, keepdims=True)
            put_heads(out, tile, first, (dot(vt, p.astype(jnp.bfloat16), NN) / total).T)
            row = top + jnp.log2(total)
            for n in range(HP):
                lse[0, tile, first + n : first + n + 1, :] = row[:, n * TILE : (n + 1) * TILE]

        over_heads(step)


def backward_kernel(q, k2, v2, s2, k1, v1, s1, k0, v0, s0, segq, out, lse, cot, *rest):
    dq, own, send1, send2, pt_ref, dst_ref, dk_ref, dv_ref = rest[-8:]
    for tile in range(ROWS // TILE):
        k = band((k2, k1, k0), tile * TILE)
        v = band((v2, v1, v0), tile * TILE)
        kt = k.T
        bias = bias_of((s2, s1, s0), segq, tile)

        def step(first):
            cols = slice(first * TILE, (first + HP) * TILE)
            ch = heads_of(cot, tile, first)
            oh = heads_of(out, tile, first)
            delta = jnp.sum(
                (ch.astype(jnp.float32) * oh.astype(jnp.float32)).T, axis=0, keepdims=True
            )
            row = jnp.concatenate(
                [lse[0, tile, first + n : first + n + 1, :] for n in range(HP)], axis=1
            )
            x = dot(k, heads_of(q, tile, first), NT) * (SCALE * LOG2E) + bias
            p = jnp.exp2(x - row)
            pt_ref[:, cols] = p.astype(jnp.bfloat16)
            ds = (p * (dot(v, ch, NT) - delta)).astype(jnp.bfloat16)
            dst_ref[:, cols] = ds
            put_heads(dq, tile, first, (dot(kt, ds, NN) * SCALE).T)

        over_heads(step)
        dv = dot(pt_ref[...], heads_of(cot, tile, 0, GROUP), NN)
        dk = dot(dst_ref[...], heads_of(q, tile, 0, GROUP), NN) * SCALE
        if tile == 0:
            dv_ref[:BAND] = dv
            dk_ref[:BAND] = dk
            dv_ref[BAND:] = jnp.zeros((WINDOW - BAND, DIM), jnp.float32)
            dk_ref[BAND:] = jnp.zeros((WINDOW - BAND, DIM), jnp.float32)
        else:
            dv_ref[WINDOW - BAND :] += dv
            dk_ref[WINDOW - BAND :] += dk
    for n, ref in enumerate((send2, send1, own)):
        rows = slice(n * ROWS, (n + 1) * ROWS)
        ref[0] = dk_ref[rows].astype(ref.dtype)
        ref[1] = dv_ref[rows].astype(ref.dtype)


def kv_specs(start):
    k = pl.BlockSpec((ROWS, DIM), lambda g: (0, g + start))
    v = pl.BlockSpec((ROWS, DIM), lambda g: (0, g + start + KV_HEADS))
    s = pl.BlockSpec((ROWS, DIM), lambda g: (0, 2 * KV_HEADS))
    return [k, v, s] * 3


def wide(start):
    return pl.BlockSpec((ROWS, GROUP * DIM), lambda g: (0, g + start))


SEGQ = pl.BlockSpec((1, ROWS), lambda g: (0, 0))


def lse_spec(start):
    return pl.BlockSpec((1, ROWS // TILE, GROUP, TILE), lambda g: (g + start, 0, 0, 0))


def cost(groups, dots=5):
    elements = groups * GROUP * ROWS * BAND
    return pl.CostEstimate(
        flops=2 * DIM * elements * dots, transcendentals=elements, bytes_accessed=groups * 1000
    )


def forward(q, blocks, segq, start, groups):
    b2, b1, b0 = blocks
    return pl.pallas_call(
        forward_kernel,
        grid=(groups,),
        in_specs=[wide(start), *kv_specs(start), SEGQ],
        out_specs=[wide(0), lse_spec(0)],
        out_shape=[
            jax.ShapeDtypeStruct((ROWS, groups * GROUP * DIM), jnp.bfloat16),
            jax.ShapeDtypeStruct((groups, ROWS // TILE, GROUP, TILE), jnp.float32),
        ],
        compiler_params=pltpu.CompilerParams(vmem_limit_bytes=VMEM),
        cost_estimate=cost(groups),
        name="attention_forward",
    )(q, b2, b2, b2, b1, b1, b1, b0, b0, b0, segq)


def backward(q, blocks, segq, out, lse, cot, grad_q, start, groups):
    b2, b1, b0 = blocks
    part = jax.ShapeDtypeStruct((2, ROWS, groups * DIM), jnp.bfloat16)
    part_spec = pl.BlockSpec((2, ROWS, DIM), lambda g: (0, 0, g))
    args = [q, b2, b2, b2, b1, b1, b1, b0, b0, b0, segq, out, lse, cot]
    in_specs = [wide(start), *kv_specs(start), SEGQ, wide(0), lse_spec(0), wide(start)]
    aliases = {}
    if grad_q is not None:
        aliases = {len(args): 0}
        args.append(grad_q)
        in_specs.append(pl.BlockSpec(memory_space=pl.ANY))
    return pl.pallas_call(
        backward_kernel,
        grid=(groups,),
        in_specs=in_specs,
        out_specs=[wide(start), part_spec, part_spec, part_spec],
        out_shape=[
            jax.ShapeDtypeStruct((ROWS, HEADS * DIM), jnp.bfloat16),
            jax.ShapeDtypeStruct((2, ROWS, groups * DIM), jnp.float32),
            part,
            part,
        ],
        scratch_shapes=[
            pltpu.VMEM((BAND, GROUP * TILE), jnp.bfloat16),
            pltpu.VMEM((BAND, GROUP * TILE), jnp.bfloat16),
            pltpu.VMEM((WINDOW, DIM), jnp.float32),
            pltpu.VMEM((WINDOW, DIM), jnp.float32),
        ],
        input_output_aliases=aliases,
        compiler_params=pltpu.CompilerParams(vmem_limit_bytes=VMEM),
        cost_estimate=cost(groups),
        name="attention_backward",
    )(*args)


def place_kernel(part, *rest):
    rest[-1][...] = part[...]


def place(part, whole, start, after):
    rows = ROWS // 2
    spec = lambda first: pl.BlockSpec((rows, GROUP * DIM), lambda c, r: (r, c + first))
    args, in_specs, aliases = [part, after], [spec(0), pl.BlockSpec(memory_space=pl.ANY)], {}
    if whole is not None:
        args.append(whole)
        in_specs.append(pl.BlockSpec(memory_space=pl.ANY))
        aliases = {2: 0}
    return pl.pallas_call(
        place_kernel,
        grid=(part.shape[1] // (GROUP * DIM), 2),
        in_specs=in_specs,
        out_specs=spec(start),
        out_shape=jax.ShapeDtypeStruct((ROWS, HEADS * DIM), jnp.bfloat16),
        input_output_aliases=aliases,
        cost_estimate=pl.CostEstimate(
            flops=0, transcendentals=0, bytes_accessed=4 * ROWS * part.shape[1]
        ),
        name="place_columns",
    )(*args)


def combine_kernel(*refs):
    n = len(PARTS)
    parts, (grad_k, grad_v, sums, sems) = refs[: 3 * n], refs[3 * n :]
    for (start, groups), own, one, two in zip(PARTS, parts[:n], parts[n : 2 * n], parts[2 * n :]):
        total = own[...] + one[...].astype(jnp.float32) + two[...].astype(jnp.float32)
        sums[:, :, start * DIM : (start + groups) * DIM] = total.astype(jnp.bfloat16)
    copies = [
        pltpu.make_async_copy(sums.at[i], out, sems.at[i]) for i, out in enumerate((grad_k, grad_v))
    ]
    for copy in copies:
        copy.start()
    for copy in copies:
        copy.wait()


def combine(own, one, two):
    out = jax.ShapeDtypeStruct((ROWS, KV_COLS), jnp.bfloat16)
    return pl.pallas_call(
        combine_kernel,
        in_specs=[pl.BlockSpec(memory_space=pltpu.VMEM)] * (3 * len(PARTS)),
        out_specs=[pl.BlockSpec(memory_space=pltpu.HBM)] * 2,
        out_shape=[out, out],
        scratch_shapes=[
            pltpu.VMEM((2, ROWS, KV_COLS), jnp.bfloat16),
            pltpu.SemaphoreType.DMA((2,)),
        ],
        compiler_params=pltpu.CompilerParams(vmem_limit_bytes=VMEM),
        cost_estimate=pl.CostEstimate(flops=1000, transcendentals=0, bytes_accessed=1000),
        name="combine_gradients",
    )(*own, *one, *two)


def shifted(array, by):
    n = lax.axis_size("ctx")
    return lax.ppermute(array, "ctx", [(c, c + by) for c in range(n) if 0 <= c + by < n])


def branch(shift_bit, q, k, v, seg, out_grad):
    pairs = [(i, i ^ 1 << shift_bit) for i in range(lax.axis_size("dp"))]
    swap = lambda array: lax.ppermute(array, "dp", pairs)
    cot = swap(out_grad)
    segk = jnp.broadcast_to((seg + 1).astype(jnp.bfloat16).reshape(ROWS, 1), (ROWS, DIM))
    b0 = jnp.concatenate([k, v, segk], axis=1)
    blocks = (shifted(b0, 2), shifted(b0, 1), b0)
    segq = (seg + 1).astype(jnp.float32)
    outs = [forward(q, blocks, segq, *part) for part in PARTS]
    swapped = [swap(out) for out, _ in outs]
    grad_q, own, one, two = None, [], [], []
    for (out, lse), part in zip(outs, PARTS):
        grad_q, mine, send1, send2 = backward(q, blocks, segq, out, lse, cot, grad_q, *part)
        own.append(mine)
        one.append(shifted(send1, -1))
        two.append(shifted(send2, -2))
    grad_k, grad_v = combine(own, one, two)
    attn_out = None
    for landed, (start, _) in zip(swapped, PARTS):
        attn_out = place(landed, attn_out, start, grad_k)
    return attn_out, grad_q, grad_k, grad_v


def local(queries, keys, values, segment_ids, out_grad, partner_bit):
    outs = lax.switch(
        partner_bit[0],
        [partial(branch, shift_bit) for shift_bit in range(3)],
        queries[0],
        keys[0],
        values[0],
        segment_ids,
        out_grad[0],
    )
    return tuple(out[None] for out in outs)


def solution(mesh):
    split = P("dp", "ctx", None)
    return jax.shard_map(
        local,
        mesh=mesh,
        in_specs=(split, split, split, P("dp", "ctx"), split, P()),
        out_specs=(split,) * 4,
        check_vma=False,
    )
```

```python
from functools import partial

import jax
import jax.numpy as jnp
from jax import lax
from jax.experimental import pallas as pl
from jax.experimental.pallas import tpu as pltpu
from jax.sharding import PartitionSpec as P

HEADS = 32
KV_HEADS = 4
GROUP = HEADS // KV_HEADS
DIM = 128
ROWS = 256
TILE = 128
BAND = 640
WINDOW = 768
HP = 2
COST = 4
FWD_UNROLL = 2
BWD_UNROLL = 2
KV_COLS = KV_HEADS * DIM
LOG2E = 1.4426950408889634
SCALE = DIM**-0.5
MASKED = -1e30
PARTS = ((0, 3), (3, 1))
WHOLE = ((0, KV_HEADS),)
COPIES = 8
LATE = (2,)
VMEM = 48 * 1024 * 1024

NT = (((1,), (1,)), ((), ()))
NN = (((1,), (0,)), ((), ()))


def dot(a, b, dims):
    return lax.dot_general(a, b, dims, preferred_element_type=jnp.float32)


def fill_window(refs, seg, window):
    k2, v2, s2, k1, v1, s1, k1x, v1x, s1x, k0, v0, s0 = refs
    for n, (two, one, other, own) in enumerate(((k2, k1, k1x, k0), (v2, v1, v1x, v0))):
        window[n, 0:ROWS] = two[...]
        window[n, ROWS : 2 * ROWS] = one[...] + other[...]
        window[n, 2 * ROWS :] = own[...]
    seg[0:ROWS] = s2[...].astype(jnp.float32)
    seg[ROWS : 2 * ROWS] = (s1[...] + s1x[...]).astype(jnp.float32)
    seg[2 * ROWS :] = s0[...].astype(jnp.float32)


def bias_of(seg, segq, tile):
    segk = seg[pl.ds(pl.multiple_of(tile * TILE, TILE), BAND)]
    first = segq[:, :TILE]
    second = segq[:, TILE:]
    key = lax.broadcasted_iota(jnp.int32, (BAND, TILE), 0)
    query = lax.broadcasted_iota(jnp.int32, (BAND, TILE), 1) + (BAND - TILE)
    ok = (segk == jnp.where(tile == 0, first, second)) & (key <= query)
    bias = jnp.where(ok, jnp.float32(0.0), jnp.float32(MASKED))
    return jnp.concatenate([bias] * HP, axis=1)


def tile_rows(tile):
    return pl.ds(pl.multiple_of(tile * TILE, TILE), TILE)


def head_cols(head, count=1):
    return pl.ds(pl.multiple_of(head * DIM, DIM), count * DIM)


def stacked(value):
    heads = value.shape[1] // DIM
    return jnp.concatenate([value[:, n * DIM : (n + 1) * DIM] for n in range(heads)], axis=0)


def unstacked(value):
    heads = value.shape[0] // TILE
    return jnp.concatenate([value[n * TILE : (n + 1) * TILE] for n in range(heads)], axis=1)


def over_heads(step, unroll):
    def trip(n, carry):
        for m in range(unroll):
            step((n * unroll + m) * HP)
        return carry

    lax.fori_loop(0, GROUP // (HP * unroll), trip, 0)


def forward_kernel(q, *rest):
    blocks, (segq, out, lse, window, seg) = rest[:12], rest[12:]
    tile = pl.program_id(1)

    @pl.when(tile == 0)
    def _():
        fill_window(blocks, seg, window)

    rows = pl.ds(pl.multiple_of(tile * TILE, TILE), BAND)
    k = window[0, rows]
    vt = window[1, rows].T
    bias = bias_of(seg, segq[...], tile)

    def step(first):
        x = dot(k, stacked(q[:, head_cols(first, HP)]), NT) * (SCALE * LOG2E) + bias
        top = jnp.max(x, axis=0, keepdims=True)
        p = jnp.exp2(x - top)
        total = jnp.sum(p, axis=0, keepdims=True)
        o = (dot(vt, p.astype(jnp.bfloat16), NN) / total).T
        out[:, head_cols(first, HP)] = unstacked(o).astype(jnp.bfloat16)
        row = top + jnp.log2(total)
        for n in range(HP):
            lse[0, 0, pl.ds(first + n, 1), :] = row[:, n * TILE : (n + 1) * TILE]

    over_heads(step, FWD_UNROLL)


def backward_kernel(q, *rest):
    blocks, (segq, out, lse, cot) = rest[:12], rest[12:16]
    dq, own, send1, send2, window, seg, pt_ref, dst_ref, dk_ref, dv_ref = rest[-10:]
    tile = pl.program_id(1)

    @pl.when(tile == 0)
    def _():
        fill_window(blocks, seg, window)
        dk_ref[...] = jnp.zeros_like(dk_ref)
        dv_ref[...] = jnp.zeros_like(dv_ref)

    rows = pl.ds(pl.multiple_of(tile * TILE, TILE), BAND)
    k = window[0, rows]
    v = window[1, rows]
    kt = k.T
    bias = bias_of(seg, segq[...], tile)

    def step(first):
        heads = head_cols(first, HP)
        ch = stacked(cot[:, heads])
        oh = stacked(out[:, heads])
        delta = jnp.sum((ch.astype(jnp.float32) * oh.astype(jnp.float32)).T, axis=0, keepdims=True)
        row = jnp.concatenate([lse[0, 0, pl.ds(first + n, 1), :] for n in range(HP)], axis=1)
        x = dot(k, stacked(q[:, heads]), NT) * (SCALE * LOG2E) + bias
        p = jnp.exp2(x - row)
        pt_ref[:, heads] = p.astype(jnp.bfloat16)
        ds = (p * (dot(v, ch, NT) - delta)).astype(jnp.bfloat16)
        dst_ref[:, heads] = ds
        dq[:, heads] = unstacked((dot(kt, ds, NN) * SCALE).T).astype(jnp.bfloat16)

    over_heads(step, BWD_UNROLL)
    dv_ref[rows] += dot(pt_ref[...], stacked(cot[...]), NN)
    dk_ref[rows] += dot(dst_ref[...], stacked(q[...]), NN) * SCALE

    @pl.when(tile == ROWS // TILE - 1)
    def _():
        for n, ref in enumerate((send2, send1, own)):
            part = slice(n * ROWS, (n + 1) * ROWS)
            ref[0] = dk_ref[part].astype(ref.dtype)
            ref[1] = dv_ref[part].astype(ref.dtype)


def kv_specs(start):
    k = pl.BlockSpec((ROWS, DIM), lambda g, t: (0, g + start))
    v = pl.BlockSpec((ROWS, DIM), lambda g, t: (0, g + start + KV_HEADS))
    s = pl.BlockSpec((ROWS, DIM), lambda g, t: (0, 2 * KV_HEADS))
    return [k, v, s] * 4


def wide(start):
    return pl.BlockSpec((TILE, GROUP * DIM), lambda g, t: (t, g + start))


def lse_spec(start):
    return pl.BlockSpec((1, 1, GROUP, TILE), lambda g, t: (g + start, t, 0, 0))


SEGQ = pl.BlockSpec((1, ROWS), lambda g, t: (0, 0))
WINDOWS = [
    pltpu.VMEM((2, WINDOW, DIM), jnp.bfloat16),
    pltpu.VMEM((WINDOW, DIM), jnp.float32),
]


def cost(groups, dots):
    elements = groups * GROUP * ROWS * BAND
    return pl.CostEstimate(
        flops=COST * DIM * elements * dots, transcendentals=COST * elements // 2, bytes_accessed=1000
    )


def forward(q, blocks, segq):
    return pl.pallas_call(
        forward_kernel,
        grid=(KV_HEADS, ROWS // TILE),
        in_specs=[wide(0), *kv_specs(0), SEGQ],
        out_specs=[wide(0), lse_spec(0)],
        out_shape=[
            jax.ShapeDtypeStruct((ROWS, HEADS * DIM), jnp.bfloat16),
            jax.ShapeDtypeStruct((KV_HEADS, ROWS // TILE, GROUP, TILE), jnp.float32),
        ],
        scratch_shapes=WINDOWS,
        compiler_params=pltpu.CompilerParams(vmem_limit_bytes=VMEM),
        cost_estimate=pl.CostEstimate(flops=1000, transcendentals=0, bytes_accessed=1000),
        name="attention_forward",
    )(q, *(block for block in blocks for _ in range(3)), segq)


def backward(q, blocks, segq, out, lse, cot, grad_q, start, groups):
    part = jax.ShapeDtypeStruct((2, ROWS, groups * DIM), jnp.bfloat16)
    part_spec = pl.BlockSpec((2, ROWS, DIM), lambda g, t: (0, 0, g))
    args = [q, *(block for block in blocks for _ in range(3)), segq, out, lse, cot]
    in_specs = [wide(start), *kv_specs(start), SEGQ, wide(start), lse_spec(start), wide(start)]
    aliases = {}
    if grad_q is not None:
        aliases = {len(args): 0}
        args.append(grad_q)
        in_specs.append(pl.BlockSpec(memory_space=pltpu.HBM))
    return pl.pallas_call(
        backward_kernel,
        grid=(groups, ROWS // TILE),
        in_specs=in_specs,
        out_specs=[wide(start), part_spec, part_spec, part_spec],
        out_shape=[
            jax.ShapeDtypeStruct((ROWS, HEADS * DIM), jnp.bfloat16),
            jax.ShapeDtypeStruct((2, ROWS, groups * DIM), jnp.float32),
            part,
            part,
        ],
        scratch_shapes=[
            *WINDOWS,
            pltpu.VMEM((BAND, GROUP * TILE), jnp.bfloat16),
            pltpu.VMEM((BAND, GROUP * TILE), jnp.bfloat16),
            pltpu.VMEM((WINDOW, DIM), jnp.float32),
            pltpu.VMEM((WINDOW, DIM), jnp.float32),
        ],
        input_output_aliases=aliases,
        compiler_params=pltpu.CompilerParams(vmem_limit_bytes=VMEM),
        cost_estimate=cost(groups, 5),
        name="attention_backward",
    )(*args)


def finish_kernel(parts, landed, *refs):
    *terms, attn_out, grad_k, grad_v, sums, sems = refs
    rows = ROWS // COPIES
    copies = [
        pltpu.make_async_copy(
            landed.at[n * rows : (n + 1) * rows], attn_out.at[n * rows : (n + 1) * rows], sems.at[n]
        )
        for n in range(COPIES)
    ]
    for copy in copies:
        copy.start()
    for n, (start, groups) in enumerate(parts):
        own, one, two = terms[3 * n : 3 * n + 3]
        total = own[...] + one[...].astype(jnp.float32) + two[...].astype(jnp.float32)
        sums[:, :, start * DIM : (start + groups) * DIM] = total.astype(jnp.bfloat16)
    more = [
        pltpu.make_async_copy(sums.at[i], out, sems.at[COPIES + i])
        for i, out in enumerate((grad_k, grad_v))
    ]
    for copy in more:
        copy.start()
    for copy in copies + more:
        copy.wait()


def finish(parts, landed, terms):
    hbm = pl.BlockSpec(memory_space=pltpu.HBM)
    out = jax.ShapeDtypeStruct((ROWS, KV_COLS), jnp.bfloat16)
    return pl.pallas_call(
        partial(finish_kernel, parts),
        in_specs=[hbm] + [pl.BlockSpec(memory_space=pltpu.VMEM)] * (3 * len(parts)),
        out_specs=[hbm] * 3,
        out_shape=[jax.ShapeDtypeStruct(landed.shape, landed.dtype), out, out],
        scratch_shapes=[
            pltpu.VMEM((2, ROWS, KV_COLS), jnp.bfloat16),
            pltpu.SemaphoreType.DMA((COPIES + 2,)),
        ],
        compiler_params=pltpu.CompilerParams(vmem_limit_bytes=VMEM),
        cost_estimate=pl.CostEstimate(flops=1000, transcendentals=0, bytes_accessed=1000),
        name="finish_outputs",
    )(landed, *(array for part in terms for array in part))


def shifted(array, pairs):
    return lax.ppermute(array, "ctx", pairs)


def branch(shift_bit, q, k, v, seg, out_grad):
    pairs = [(i, i ^ 1 << shift_bit) for i in range(lax.axis_size("dp"))]
    swap = lambda array: lax.ppermute(array, "dp", pairs)
    cot = swap(out_grad)
    segk = jnp.broadcast_to((seg + 1).astype(jnp.bfloat16).reshape(ROWS, 1), (ROWS, DIM))
    b0 = jnp.concatenate([k, v, segk], axis=1)
    two = shifted(b0, [(0, 2), (1, 3)])
    blocks = (two, shifted(b0, [(0, 1), (2, 3)]), shifted(two, [(3, 2)]), b0)
    segq = (seg + 1).astype(jnp.float32)
    out, lse = forward(q, blocks, segq)
    to_send = out
    if shift_bit in LATE:
        to_send, cot = lax.optimization_barrier((out, cot))
    landed = swap(to_send)
    grad_q, terms = None, []
    parts = WHOLE if shift_bit in LATE else PARTS
    for part in parts:
        grad_q, own, send1, send2 = backward(q, blocks, segq, out, lse, cot, grad_q, *part)
        if shift_bit in LATE:
            place = lax.axis_index("ctx")
            came = shifted(send1, [(1, 0), (2, 3), (3, 2)])
            none = jnp.zeros_like(came)
            two = shifted(send2 + jnp.where(place == 3, came, none), [(2, 0), (3, 1)])
            one = jnp.where(place == 3, none, came)
        else:
            one = shifted(send1, [(1, 0), (2, 1), (3, 2)])
            two = shifted(send2, [(2, 0), (3, 1)])
        terms.append((own, one, two))
    attn_out, grad_k, grad_v = finish(parts, landed, terms)
    return attn_out, grad_q, grad_k, grad_v


def local(queries, keys, values, segment_ids, out_grad, partner_bit):
    outs = lax.switch(
        partner_bit[0],
        [partial(branch, shift_bit) for shift_bit in range(3)],
        queries[0],
        keys[0],
        values[0],
        segment_ids,
        out_grad[0],
    )
    return tuple(out[None] for out in outs)


def solution(mesh):
    split = P("dp", "ctx", None)
    return jax.shard_map(
        local,
        mesh=mesh,
        in_specs=(split, split, split, P("dp", "ctx"), split, P()),
        out_specs=(split,) * 4,
        check_vma=False,
    )
```

```python
from functools import partial

import jax
import jax.numpy as jnp
from jax import lax
from jax.experimental import pallas as pl
from jax.experimental.pallas import tpu as pltpu
from jax.sharding import PartitionSpec as P

HEADS = 32
KV_HEADS = 4
GROUP = HEADS // KV_HEADS
DIM = 128
ROWS = 256
TILE = 128
BAND = 640
WINDOW = 768
HP = 2
COST = 4
UNROLL = (4, 2)
UNROLL_LATE = (1, 2)
KV_COLS = KV_HEADS * DIM
LOG2E = 1.4426950408889634
SCALE = DIM**-0.5
MASKED = -1e30
PARTS = ((0, 3), (3, 1))
WHOLE = ((0, KV_HEADS),)
COPIES = 8
LATE = (2,)
VMEM = 48 * 1024 * 1024

NT = (((1,), (1,)), ((), ()))
NN = (((1,), (0,)), ((), ()))


def dot(a, b, dims):
    return lax.dot_general(a, b, dims, preferred_element_type=jnp.float32)


def fill_window(refs, seg, window):
    k2, v2, s2, k1, v1, s1, k1x, v1x, s1x, k0, v0, s0 = refs
    for n, (two, one, other, own) in enumerate(((k2, k1, k1x, k0), (v2, v1, v1x, v0))):
        window[n, 0:ROWS] = two[...]
        window[n, ROWS : 2 * ROWS] = one[...] + other[...]
        window[n, 2 * ROWS :] = own[...]
    seg[0:ROWS] = s2[...].astype(jnp.float32)
    seg[ROWS : 2 * ROWS] = (s1[...] + s1x[...]).astype(jnp.float32)
    seg[2 * ROWS :] = s0[...].astype(jnp.float32)


def bias_of(seg, segq, tile):
    segk = seg[pl.ds(pl.multiple_of(tile * TILE, TILE), BAND)]
    first = segq[:, :TILE]
    second = segq[:, TILE:]
    key = lax.broadcasted_iota(jnp.int32, (BAND, TILE), 0)
    query = lax.broadcasted_iota(jnp.int32, (BAND, TILE), 1) + (BAND - TILE)
    ok = (segk == jnp.where(tile == 0, first, second)) & (key <= query)
    bias = jnp.where(ok, jnp.float32(0.0), jnp.float32(MASKED))
    return jnp.concatenate([bias] * HP, axis=1)


def tile_rows(tile):
    return pl.ds(pl.multiple_of(tile * TILE, TILE), TILE)


def head_cols(head, count=1):
    return pl.ds(pl.multiple_of(head * DIM, DIM), count * DIM)


def stacked(value):
    heads = value.shape[1] // DIM
    return jnp.concatenate([value[:, n * DIM : (n + 1) * DIM] for n in range(heads)], axis=0)


def unstacked(value):
    heads = value.shape[0] // TILE
    return jnp.concatenate([value[n * TILE : (n + 1) * TILE] for n in range(heads)], axis=1)


def over_heads(step, unroll):
    def trip(n, carry):
        for m in range(unroll):
            step((n * unroll + m) * HP)
        return carry

    lax.fori_loop(0, GROUP // (HP * unroll), trip, 0)


def forward_kernel(unroll, q, *rest):
    blocks, (segq, out, lse, window, seg) = rest[:12], rest[12:]
    tile = pl.program_id(1)

    @pl.when(tile == 0)
    def _():
        fill_window(blocks, seg, window)

    rows = pl.ds(pl.multiple_of(tile * TILE, TILE), BAND)
    k = window[0, rows]
    vt = window[1, rows].T
    bias = bias_of(seg, segq[...], tile)

    def step(first):
        x = dot(k, stacked(q[:, head_cols(first, HP)]), NT) * (SCALE * LOG2E) + bias
        top = jnp.max(x, axis=0, keepdims=True)
        p = jnp.exp2(x - top)
        total = jnp.sum(p, axis=0, keepdims=True)
        o = (dot(vt, p.astype(jnp.bfloat16), NN) / total).T
        out[:, head_cols(first, HP)] = unstacked(o).astype(jnp.bfloat16)
        row = top + jnp.log2(total)
        for n in range(HP):
            lse[0, 0, pl.ds(first + n, 1), :] = row[:, n * TILE : (n + 1) * TILE]

    over_heads(step, unroll)


def backward_kernel(unroll, q, *rest):
    blocks, (segq, out, lse, cot) = rest[:12], rest[12:16]
    dq, own, send1, send2, window, seg, pt_ref, dst_ref, dk_ref, dv_ref = rest[-10:]
    tile = pl.program_id(1)

    @pl.when(tile == 0)
    def _():
        fill_window(blocks, seg, window)
        dk_ref[...] = jnp.zeros_like(dk_ref)
        dv_ref[...] = jnp.zeros_like(dv_ref)

    rows = pl.ds(pl.multiple_of(tile * TILE, TILE), BAND)
    k = window[0, rows]
    v = window[1, rows]
    kt = k.T
    bias = bias_of(seg, segq[...], tile)

    def step(first):
        heads = head_cols(first, HP)
        ch = stacked(cot[:, heads])
        oh = stacked(out[:, heads])
        delta = jnp.sum((ch.astype(jnp.float32) * oh.astype(jnp.float32)).T, axis=0, keepdims=True)
        row = jnp.concatenate([lse[0, 0, pl.ds(first + n, 1), :] for n in range(HP)], axis=1)
        x = dot(k, stacked(q[:, heads]), NT) * (SCALE * LOG2E) + bias
        p = jnp.exp2(x - row)
        pt_ref[:, heads] = p.astype(jnp.bfloat16)
        ds = (p * (dot(v, ch, NT) - delta)).astype(jnp.bfloat16)
        dst_ref[:, heads] = ds
        dq[:, heads] = unstacked((dot(kt, ds, NN) * SCALE).T).astype(jnp.bfloat16)

    over_heads(step, unroll)
    dv_ref[rows] += dot(pt_ref[...], stacked(cot[...]), NN)
    dk_ref[rows] += dot(dst_ref[...], stacked(q[...]), NN) * SCALE

    @pl.when(tile == ROWS // TILE - 1)
    def _():
        for n, ref in enumerate((send2, send1, own)):
            part = slice(n * ROWS, (n + 1) * ROWS)
            ref[0] = dk_ref[part].astype(ref.dtype)
            ref[1] = dv_ref[part].astype(ref.dtype)


def kv_specs(start):
    k = pl.BlockSpec((ROWS, DIM), lambda g, t: (0, g + start))
    v = pl.BlockSpec((ROWS, DIM), lambda g, t: (0, g + start + KV_HEADS))
    s = pl.BlockSpec((ROWS, DIM), lambda g, t: (0, 2 * KV_HEADS))
    return [k, v, s] * 4


def wide(start):
    return pl.BlockSpec((TILE, GROUP * DIM), lambda g, t: (t, g + start))


def lse_spec(start):
    return pl.BlockSpec((1, 1, GROUP, TILE), lambda g, t: (g + start, t, 0, 0))


SEGQ = pl.BlockSpec((1, ROWS), lambda g, t: (0, 0))
WINDOWS = [
    pltpu.VMEM((2, WINDOW, DIM), jnp.bfloat16),
    pltpu.VMEM((WINDOW, DIM), jnp.float32),
]


def cost(groups, dots):
    elements = groups * GROUP * ROWS * BAND
    return pl.CostEstimate(
        flops=COST * DIM * elements * dots, transcendentals=COST * elements // 2, bytes_accessed=1000
    )


def forward(unroll, q, blocks, segq):
    return pl.pallas_call(
        partial(forward_kernel, unroll),
        grid=(KV_HEADS, ROWS // TILE),
        in_specs=[wide(0), *kv_specs(0), SEGQ],
        out_specs=[wide(0), lse_spec(0)],
        out_shape=[
            jax.ShapeDtypeStruct((ROWS, HEADS * DIM), jnp.bfloat16),
            jax.ShapeDtypeStruct((KV_HEADS, ROWS // TILE, GROUP, TILE), jnp.float32),
        ],
        scratch_shapes=WINDOWS,
        compiler_params=pltpu.CompilerParams(vmem_limit_bytes=VMEM),
        cost_estimate=pl.CostEstimate(flops=1000, transcendentals=0, bytes_accessed=1000),
        name="attention_forward",
    )(q, *(block for block in blocks for _ in range(3)), segq)


def backward(unroll, q, blocks, segq, out, lse, cot, grad_q, start, groups):
    part = jax.ShapeDtypeStruct((2, ROWS, groups * DIM), jnp.bfloat16)
    part_spec = pl.BlockSpec((2, ROWS, DIM), lambda g, t: (0, 0, g))
    args = [q, *(block for block in blocks for _ in range(3)), segq, out, lse, cot]
    in_specs = [wide(start), *kv_specs(start), SEGQ, wide(start), lse_spec(start), wide(start)]
    aliases = {}
    if grad_q is not None:
        aliases = {len(args): 0}
        args.append(grad_q)
        in_specs.append(pl.BlockSpec(memory_space=pltpu.HBM))
    return pl.pallas_call(
        partial(backward_kernel, unroll),
        grid=(groups, ROWS // TILE),
        in_specs=in_specs,
        out_specs=[wide(start), part_spec, part_spec, part_spec],
        out_shape=[
            jax.ShapeDtypeStruct((ROWS, HEADS * DIM), jnp.bfloat16),
            jax.ShapeDtypeStruct((2, ROWS, groups * DIM), jnp.float32),
            part,
            part,
        ],
        scratch_shapes=[
            *WINDOWS,
            pltpu.VMEM((BAND, GROUP * TILE), jnp.bfloat16),
            pltpu.VMEM((BAND, GROUP * TILE), jnp.bfloat16),
            pltpu.VMEM((WINDOW, DIM), jnp.float32),
            pltpu.VMEM((WINDOW, DIM), jnp.float32),
        ],
        input_output_aliases=aliases,
        compiler_params=pltpu.CompilerParams(vmem_limit_bytes=VMEM),
        cost_estimate=cost(groups, 5),
        name="attention_backward",
    )(*args)


def finish_kernel(parts, landed, *refs):
    *terms, attn_out, grad_k, grad_v, sums, sems = refs
    rows = ROWS // COPIES
    copies = [
        pltpu.make_async_copy(
            landed.at[n * rows : (n + 1) * rows], attn_out.at[n * rows : (n + 1) * rows], sems.at[n]
        )
        for n in range(COPIES)
    ]
    for copy in copies:
        copy.start()
    for n, (start, groups) in enumerate(parts):
        own, one, two = terms[3 * n : 3 * n + 3]
        total = own[...] + one[...].astype(jnp.float32) + two[...].astype(jnp.float32)
        sums[:, :, start * DIM : (start + groups) * DIM] = total.astype(jnp.bfloat16)
    more = [
        pltpu.make_async_copy(sums.at[i], out, sems.at[COPIES + i])
        for i, out in enumerate((grad_k, grad_v))
    ]
    for copy in more:
        copy.start()
    for copy in copies + more:
        copy.wait()


def finish(parts, landed, terms):
    hbm = pl.BlockSpec(memory_space=pltpu.HBM)
    out = jax.ShapeDtypeStruct((ROWS, KV_COLS), jnp.bfloat16)
    return pl.pallas_call(
        partial(finish_kernel, parts),
        in_specs=[hbm] + [pl.BlockSpec(memory_space=pltpu.VMEM)] * (3 * len(parts)),
        out_specs=[hbm] * 3,
        out_shape=[jax.ShapeDtypeStruct(landed.shape, landed.dtype), out, out],
        scratch_shapes=[
            pltpu.VMEM((2, ROWS, KV_COLS), jnp.bfloat16),
            pltpu.SemaphoreType.DMA((COPIES + 2,)),
        ],
        compiler_params=pltpu.CompilerParams(vmem_limit_bytes=VMEM),
        cost_estimate=pl.CostEstimate(flops=1000, transcendentals=0, bytes_accessed=1000),
        name="finish_outputs",
    )(landed, *(array for part in terms for array in part))


def shifted(array, pairs):
    return lax.ppermute(array, "ctx", pairs)


def branch(shift_bit, q, k, v, seg, out_grad):
    pairs = [(i, i ^ 1 << shift_bit) for i in range(lax.axis_size("dp"))]
    swap = lambda array: lax.ppermute(array, "dp", pairs)
    cot = swap(out_grad)
    segk = jnp.broadcast_to((seg + 1).astype(jnp.bfloat16).reshape(ROWS, 1), (ROWS, DIM))
    b0 = jnp.concatenate([k, v, segk], axis=1)
    two = shifted(b0, [(0, 2), (1, 3)])
    blocks = (two, shifted(b0, [(0, 1), (2, 3)]), shifted(two, [(3, 2)]), b0)
    segq = (seg + 1).astype(jnp.float32)
    late = shift_bit in LATE
    forward_unroll, backward_unroll = UNROLL_LATE if late else UNROLL
    out, lse = forward(forward_unroll, q, blocks, segq)
    to_send = out
    if late:
        to_send, cot = lax.optimization_barrier((out, cot))
    landed = swap(to_send)
    grad_q, terms = None, []
    parts = WHOLE if late else PARTS
    for part in parts:
        grad_q, own, send1, send2 = backward(
            backward_unroll, q, blocks, segq, out, lse, cot, grad_q, *part
        )
        if late:
            place = lax.axis_index("ctx")
            came = shifted(send1, [(1, 0), (2, 3), (3, 2)])
            none = jnp.zeros_like(came)
            two = shifted(send2 + jnp.where(place == 3, came, none), [(2, 0), (3, 1)])
            one = jnp.where(place == 3, none, came)
        else:
            one = shifted(send1, [(1, 0), (2, 1), (3, 2)])
            two = shifted(send2, [(2, 0), (3, 1)])
        terms.append((own, one, two))
    attn_out, grad_k, grad_v = finish(parts, landed, terms)
    return attn_out, grad_q, grad_k, grad_v


def local(queries, keys, values, segment_ids, out_grad, partner_bit):
    outs = lax.switch(
        partner_bit[0],
        [partial(branch, shift_bit) for shift_bit in range(3)],
        queries[0],
        keys[0],
        values[0],
        segment_ids,
        out_grad[0],
    )
    return tuple(out[None] for out in outs)


def solution(mesh):
    split = P("dp", "ctx", None)
    return jax.shard_map(
        local,
        mesh=mesh,
        in_specs=(split, split, split, P("dp", "ctx"), split, P()),
        out_specs=(split,) * 4,
        check_vma=False,
    )
```

```python
from functools import partial

import jax
import jax.numpy as jnp
from jax import lax
from jax.experimental import pallas as pl
from jax.experimental.pallas import tpu as pltpu
from jax.sharding import PartitionSpec as P

HEADS = 32
KV_HEADS = 4
GROUP = HEADS // KV_HEADS
DIM = 128
ROWS = 256
TILE = 128
BAND = 640
WINDOW = 768
HP = 2
COST = 4
UNROLL = (4, 4)
UNROLL_LATE = (1, 2)
KV_COLS = KV_HEADS * DIM
LOG2E = 1.4426950408889634
SCALE = DIM**-0.5
MASKED = -1e30
PARTS = ((0, 3), (3, 1))
WHOLE = ((0, KV_HEADS),)
COPIES = 8
LATE = (2,)
VMEM = 48 * 1024 * 1024

NT = (((1,), (1,)), ((), ()))
NN = (((1,), (0,)), ((), ()))


def dot(a, b, dims):
    return lax.dot_general(a, b, dims, preferred_element_type=jnp.float32)


def fill_window(refs, seg, window):
    k2, v2, s2, k1, v1, s1, k1x, v1x, s1x, k0, v0, s0 = refs
    for n, (two, one, other, own) in enumerate(((k2, k1, k1x, k0), (v2, v1, v1x, v0))):
        window[n, 0:ROWS] = two[...]
        window[n, ROWS : 2 * ROWS] = one[...] + other[...]
        window[n, 2 * ROWS :] = own[...]
    seg[0:ROWS] = s2[...].astype(jnp.float32)
    seg[ROWS : 2 * ROWS] = (s1[...] + s1x[...]).astype(jnp.float32)
    seg[2 * ROWS :] = s0[...].astype(jnp.float32)


def bias_of(seg, segq, tile):
    segk = seg[pl.ds(pl.multiple_of(tile * TILE, TILE), BAND)]
    first = segq[:, :TILE]
    second = segq[:, TILE:]
    key = lax.broadcasted_iota(jnp.int32, (BAND, TILE), 0)
    query = lax.broadcasted_iota(jnp.int32, (BAND, TILE), 1) + (BAND - TILE)
    ok = (segk == jnp.where(tile == 0, first, second)) & (key <= query)
    bias = jnp.where(ok, jnp.float32(0.0), jnp.float32(MASKED))
    return jnp.concatenate([bias] * HP, axis=1)


def tile_rows(tile):
    return pl.ds(pl.multiple_of(tile * TILE, TILE), TILE)


def head_cols(head, count=1):
    return pl.ds(pl.multiple_of(head * DIM, DIM), count * DIM)


def stacked(value):
    heads = value.shape[1] // DIM
    return jnp.concatenate([value[:, n * DIM : (n + 1) * DIM] for n in range(heads)], axis=0)


def unstacked(value):
    heads = value.shape[0] // TILE
    return jnp.concatenate([value[n * TILE : (n + 1) * TILE] for n in range(heads)], axis=1)


def over_heads(step, unroll):
    def trip(n, carry):
        for m in range(unroll):
            step((n * unroll + m) * HP)
        return carry

    lax.fori_loop(0, GROUP // (HP * unroll), trip, 0)


def forward_kernel(unroll, q, *rest):
    blocks, (segq, out, lse, window, seg) = rest[:12], rest[12:]
    tile = pl.program_id(1)

    @pl.when(tile == 0)
    def _():
        fill_window(blocks, seg, window)

    rows = pl.ds(pl.multiple_of(tile * TILE, TILE), BAND)
    k = window[0, rows]
    vt = window[1, rows].T
    bias = bias_of(seg, segq[...], tile)

    def step(first):
        x = dot(k, stacked(q[:, head_cols(first, HP)]), NT) * (SCALE * LOG2E) + bias
        top = jnp.max(x, axis=0, keepdims=True)
        p = jnp.exp2(x - top)
        total = jnp.sum(p, axis=0, keepdims=True)
        o = (dot(vt, p.astype(jnp.bfloat16), NN) / total).T
        out[:, head_cols(first, HP)] = unstacked(o).astype(jnp.bfloat16)
        row = top + jnp.log2(total)
        for n in range(HP):
            lse[0, 0, pl.ds(first + n, 1), :] = row[:, n * TILE : (n + 1) * TILE]

    over_heads(step, unroll)


def backward_kernel(unroll, q, *rest):
    blocks, (segq, out, lse, cot) = rest[:12], rest[12:16]
    dq, own, send1, send2, window, seg, pt_ref, dst_ref, dk_ref, dv_ref = rest[-10:]
    tile = pl.program_id(1)

    @pl.when(tile == 0)
    def _():
        fill_window(blocks, seg, window)
        dk_ref[...] = jnp.zeros_like(dk_ref)
        dv_ref[...] = jnp.zeros_like(dv_ref)

    rows = pl.ds(pl.multiple_of(tile * TILE, TILE), BAND)
    k = window[0, rows]
    v = window[1, rows]
    kt = k.T
    bias = bias_of(seg, segq[...], tile)

    def step(first):
        heads = head_cols(first, HP)
        ch = stacked(cot[:, heads])
        oh = stacked(out[:, heads])
        delta = jnp.sum((ch.astype(jnp.float32) * oh.astype(jnp.float32)).T, axis=0, keepdims=True)
        row = jnp.concatenate([lse[0, 0, pl.ds(first + n, 1), :] for n in range(HP)], axis=1)
        x = dot(k, stacked(q[:, heads]), NT) * (SCALE * LOG2E) + bias
        p = jnp.exp2(x - row)
        pt_ref[:, heads] = p.astype(jnp.bfloat16)
        ds = (p * (dot(v, ch, NT) - delta)).astype(jnp.bfloat16)
        dst_ref[:, heads] = ds
        dq[:, heads] = unstacked((dot(kt, ds, NN) * SCALE).T).astype(jnp.bfloat16)

    over_heads(step, unroll)
    dv_ref[rows] += dot(pt_ref[...], stacked(cot[...]), NN)
    dk_ref[rows] += dot(dst_ref[...], stacked(q[...]), NN) * SCALE

    @pl.when(tile == ROWS // TILE - 1)
    def _():
        for n, ref in enumerate((send2, send1, own)):
            part = slice(n * ROWS, (n + 1) * ROWS)
            ref[0] = dk_ref[part].astype(ref.dtype)
            ref[1] = dv_ref[part].astype(ref.dtype)


def kv_specs(start):
    k = pl.BlockSpec((ROWS, DIM), lambda g, t: (0, g + start))
    v = pl.BlockSpec((ROWS, DIM), lambda g, t: (0, g + start + KV_HEADS))
    s = pl.BlockSpec((ROWS, DIM), lambda g, t: (0, 2 * KV_HEADS))
    return [k, v, s] * 4


def wide(start):
    return pl.BlockSpec((TILE, GROUP * DIM), lambda g, t: (t, g + start))


def lse_spec(start):
    return pl.BlockSpec((1, 1, GROUP, TILE), lambda g, t: (g + start, t, 0, 0))


SEGQ = pl.BlockSpec((1, ROWS), lambda g, t: (0, 0))
WINDOWS = [
    pltpu.VMEM((2, WINDOW, DIM), jnp.bfloat16),
    pltpu.VMEM((WINDOW, DIM), jnp.float32),
]


def cost(groups, dots):
    elements = groups * GROUP * ROWS * BAND
    return pl.CostEstimate(
        flops=COST * DIM * elements * dots, transcendentals=COST * elements // 2, bytes_accessed=1000
    )


def forward(unroll, q, blocks, segq):
    return pl.pallas_call(
        partial(forward_kernel, unroll),
        grid=(KV_HEADS, ROWS // TILE),
        in_specs=[wide(0), *kv_specs(0), SEGQ],
        out_specs=[wide(0), lse_spec(0)],
        out_shape=[
            jax.ShapeDtypeStruct((ROWS, HEADS * DIM), jnp.bfloat16),
            jax.ShapeDtypeStruct((KV_HEADS, ROWS // TILE, GROUP, TILE), jnp.float32),
        ],
        scratch_shapes=WINDOWS,
        compiler_params=pltpu.CompilerParams(vmem_limit_bytes=VMEM),
        cost_estimate=pl.CostEstimate(flops=1000, transcendentals=0, bytes_accessed=1000),
        name="attention_forward",
    )(q, *(block for block in blocks for _ in range(3)), segq)


def backward(unroll, q, blocks, segq, out, lse, cot, grad_q, start, groups):
    part = jax.ShapeDtypeStruct((2, ROWS, groups * DIM), jnp.bfloat16)
    part_spec = pl.BlockSpec((2, ROWS, DIM), lambda g, t: (0, 0, g))
    args = [q, *(block for block in blocks for _ in range(3)), segq, out, lse, cot]
    in_specs = [wide(start), *kv_specs(start), SEGQ, wide(start), lse_spec(start), wide(start)]
    aliases = {}
    if grad_q is not None:
        aliases = {len(args): 0}
        args.append(grad_q)
        in_specs.append(pl.BlockSpec(memory_space=pltpu.HBM))
    return pl.pallas_call(
        partial(backward_kernel, unroll),
        grid=(groups, ROWS // TILE),
        in_specs=in_specs,
        out_specs=[wide(start), part_spec, part_spec, part_spec],
        out_shape=[
            jax.ShapeDtypeStruct((ROWS, HEADS * DIM), jnp.bfloat16),
            jax.ShapeDtypeStruct((2, ROWS, groups * DIM), jnp.float32),
            part,
            part,
        ],
        scratch_shapes=[
            *WINDOWS,
            pltpu.VMEM((BAND, GROUP * TILE), jnp.bfloat16),
            pltpu.VMEM((BAND, GROUP * TILE), jnp.bfloat16),
            pltpu.VMEM((WINDOW, DIM), jnp.float32),
            pltpu.VMEM((WINDOW, DIM), jnp.float32),
        ],
        input_output_aliases=aliases,
        compiler_params=pltpu.CompilerParams(vmem_limit_bytes=VMEM),
        cost_estimate=cost(groups, 5),
        name="attention_backward",
    )(*args)


def finish_kernel(parts, landed, *refs):
    *terms, attn_out, grad_k, grad_v, sums, sems = refs
    rows = ROWS // COPIES
    copies = [
        pltpu.make_async_copy(
            landed.at[n * rows : (n + 1) * rows], attn_out.at[n * rows : (n + 1) * rows], sems.at[n]
        )
        for n in range(COPIES)
    ]
    for copy in copies:
        copy.start()
    for n, (start, groups) in enumerate(parts):
        own, one, two = terms[3 * n : 3 * n + 3]
        total = own[...] + one[...].astype(jnp.float32) + two[...].astype(jnp.float32)
        sums[:, :, start * DIM : (start + groups) * DIM] = total.astype(jnp.bfloat16)
    more = [
        pltpu.make_async_copy(sums.at[i], out, sems.at[COPIES + i])
        for i, out in enumerate((grad_k, grad_v))
    ]
    for copy in more:
        copy.start()
    for copy in copies + more:
        copy.wait()


def finish(parts, landed, terms):
    hbm = pl.BlockSpec(memory_space=pltpu.HBM)
    out = jax.ShapeDtypeStruct((ROWS, KV_COLS), jnp.bfloat16)
    return pl.pallas_call(
        partial(finish_kernel, parts),
        in_specs=[hbm] + [pl.BlockSpec(memory_space=pltpu.VMEM)] * (3 * len(parts)),
        out_specs=[hbm] * 3,
        out_shape=[jax.ShapeDtypeStruct(landed.shape, landed.dtype), out, out],
        scratch_shapes=[
            pltpu.VMEM((2, ROWS, KV_COLS), jnp.bfloat16),
            pltpu.SemaphoreType.DMA((COPIES + 2,)),
        ],
        compiler_params=pltpu.CompilerParams(vmem_limit_bytes=VMEM),
        cost_estimate=pl.CostEstimate(flops=1000, transcendentals=0, bytes_accessed=1000),
        name="finish_outputs",
    )(landed, *(array for part in terms for array in part))


def shifted(array, pairs):
    return lax.ppermute(array, "ctx", pairs)


def branch(shift_bit, q, k, v, seg, out_grad):
    pairs = [(i, i ^ 1 << shift_bit) for i in range(lax.axis_size("dp"))]
    swap = lambda array: lax.ppermute(array, "dp", pairs)
    cot = swap(out_grad)
    segk = jnp.broadcast_to((seg + 1).astype(jnp.bfloat16).reshape(ROWS, 1), (ROWS, DIM))
    b0 = jnp.concatenate([k, v, segk], axis=1)
    two = shifted(b0, [(0, 2), (1, 3)])
    blocks = (two, shifted(b0, [(0, 1), (2, 3)]), shifted(two, [(3, 2)]), b0)
    segq = (seg + 1).astype(jnp.float32)
    late = shift_bit in LATE
    forward_unroll, backward_unroll = UNROLL_LATE if late else UNROLL
    out, lse = forward(forward_unroll, q, blocks, segq)
    to_send = out
    if late:
        to_send, cot = lax.optimization_barrier((out, cot))
    landed = swap(to_send)
    grad_q, terms = None, []
    parts = WHOLE if late else PARTS
    for part in parts:
        grad_q, own, send1, send2 = backward(
            backward_unroll, q, blocks, segq, out, lse, cot, grad_q, *part
        )
        if late:
            place = lax.axis_index("ctx")
            came = shifted(send1, [(1, 0), (2, 3), (3, 2)])
            none = jnp.zeros_like(came)
            two = shifted(send2 + jnp.where(place == 3, came, none), [(2, 0), (3, 1)])
            one = jnp.where(place == 3, none, came)
        else:
            one = shifted(send1, [(1, 0), (2, 1), (3, 2)])
            two = shifted(send2, [(2, 0), (3, 1)])
        terms.append((own, one, two))
    attn_out, grad_k, grad_v = finish(parts, landed, terms)
    return attn_out, grad_q, grad_k, grad_v


def local(queries, keys, values, segment_ids, out_grad, partner_bit):
    outs = lax.switch(
        partner_bit[0],
        [partial(branch, shift_bit) for shift_bit in range(3)],
        queries[0],
        keys[0],
        values[0],
        segment_ids,
        out_grad[0],
    )
    return tuple(out[None] for out in outs)


def solution(mesh):
    split = P("dp", "ctx", None)
    return jax.shard_map(
        local,
        mesh=mesh,
        in_specs=(split, split, split, P("dp", "ctx"), split, P()),
        out_specs=(split,) * 4,
        check_vma=False,
    )
```
